32 devices in a mesh: tensor: 4 (over x, core), seq: 4 (over z), dp: 2 (over y).
Axes of the slice: x: 2, y: 2, z: 4, core: 2. Of those that a mesh axis runs over, the one named last changes fastest.
Arguments:
- inputs: bfloat16 [2, 1024, 768], P('dp', 'seq'), may hold values from -6 to 6
- cotangent: float32 [2, 1024, 768], P('dp', 'seq'), may hold values from -6 to 6
- attention_norm_gain: float32 [2, 768], replicated, may hold values from 0.1 to 1.9
- attention_norm_bias: float32 [2, 768], replicated, may hold values from -3 to 3
- w_query: bfloat16 [2, 768, 768], P(None, ('seq', 'dp'), 'tensor'), may hold values from -0.21875 to 0.21875
- b_query: float32 [2, 768], P(None, 'tensor'), may hold values from -3 to 3
- w_key: bfloat16 [2, 768, 768], P(None, ('seq', 'dp'), 'tensor'), may hold values from -0.21875 to 0.21875
- w_value: bfloat16 [2, 768, 768], P(None, ('seq', 'dp'), 'tensor'), may hold values from -0.21875 to 0.21875
- b_value: float32 [2, 768], P(None, 'tensor'), may hold values from -0.6 to 0.6
- w_out: bfloat16 [2, 768, 768], P(None, ('seq', 'dp'), 'tensor'), may hold values from -0.875 to 0.875
- b_out: float32 [2, 768], replicated, may hold values from -3 to 3
- feedforward_norm_gain: float32 [2, 768], replicated, may hold values from 0.1 to 1.9
- feedforward_norm_bias: float32 [2, 768], replicated, may hold values from -3 to 3
- w_fc1: bfloat16 [2, 768, 3072], P(None, ('seq', 'dp'), 'tensor'), may hold values from -0.21875 to 0.21875
- b_fc1: float32 [2, 3072], P(None, 'tensor'), may hold values from -3 to 3
- w_fc2: bfloat16 [2, 768, 3072], P(None, ('seq', 'dp'), 'tensor'), may hold values from -0.109375 to 0.109375
- b_fc2: float32 [2, 768], replicated, may hold values from -3 to 3
Outputs:
- encoded: float32 [2, 1024, 768], P('dp', 'seq')
- grad_inputs: float32 [2, 1024, 768], P('dp', 'seq')
- grad_ln1_gain: float32 [2, 768], replicated
- grad_ln1_bias: float32 [2, 768], replicated
- grad_w_query: float32 [2, 768, 768], P(None, ('seq', 'dp'), 'tensor')
- grad_b_query: float32 [2, 768], P(None, 'tensor')
- grad_w_key: float32 [2, 768, 768], P(None, ('seq', 'dp'), 'tensor')
- grad_w_value: float32 [2, 768, 768], P(None, ('seq', 'dp'), 'tensor')
- grad_b_value: float32 [2, 768], P(None, 'tensor')
- grad_w_out: float32 [2, 768, 768], P(None, ('seq', 'dp'), 'tensor')
- grad_b_out: float32 [2, 768], replicated
- grad_ln2_gain: float32 [2, 768], replicated
- grad_ln2_bias: float32 [2, 768], replicated
- grad_w_fc1: float32 [2, 768, 3072], P(None, ('seq', 'dp'), 'tensor')
- grad_b_fc1: float32 [2, 3072], P(None, 'tensor')
- grad_w_fc2: float32 [2, 768, 3072], P(None, ('seq', 'dp'), 'tensor')
- grad_b_fc2: float32 [2, 768], replicated
The draws below stay inside these ranges and needn't reach their ends.
All inputs are finite; a program needn't handle non-finite values.
Results may differ from the reference program's by a relative error of at most 0.029.
Values may be sent and summed in bfloat16 or wider, within the bound.
A program may use at most 128 MiB of HBM per device.

```python
import jax
import jax.numpy as jnp
from jax import lax

D = 768
HEADS = 12
HEAD_DIM = 64
FF = 3072
FRAMES = 1024
LAYERS = 2
CLIPS = 2
N_TENSOR = 4


def steps_of(own_key, shape, shards, least, high):
    loudness = 1.0
    for dim, blocks in shards:
        heights = jax.random.uniform(jax.random.fold_in(jax.random.fold_in(own_key, 6), dim), (blocks,), jnp.float32, least / len(shards), high / len(shards))
        loudness = loudness * jnp.repeat(jnp.exp(heights), shape[dim] // blocks).reshape((-1,) + (1,) * (len(shape) - 1 - dim))
    return loudness


def gaussian(key, extent, scale, most, split=(), kind=jnp.bfloat16):
    drawn = scale * jax.random.normal(key, extent, jnp.float32)
    if split:
        drawn = drawn * steps_of(key, extent, split, -0.22, 0.18)
    return jnp.clip(drawn, -most, most).astype(kind)


def setup_inputs(seed: int = 0) -> dict:
    key_list = jax.random.split(jax.random.key(seed), 18)
    return {
        "inputs": gaussian(key_list[0], (CLIPS, FRAMES, D), 1.0, 6.0, ((0, 2), (1, 4))),
        "cotangent": gaussian(key_list[1], (CLIPS, FRAMES, D), 1.0, 6.0, ((0, 2), (1, 4)), jnp.float32),
        "attention_norm_gain": jnp.clip(1.0 + 0.18 * jax.random.normal(key_list[2], (LAYERS, D), jnp.float32), 0.1, 1.9),
        "attention_norm_bias": gaussian(key_list[3], (LAYERS, D), 0.5, 3.0, (), jnp.float32),
        "w_query": gaussian(key_list[4], (LAYERS, D, D), D ** -0.5, 0.21875, ((1, 8), (2, 4))),
        "b_query": gaussian(key_list[5], (LAYERS, D), 0.5, 3.0, ((1, 4),), jnp.float32),
        "w_key": gaussian(key_list[6], (LAYERS, D, D), D ** -0.5, 0.21875, ((1, 8), (2, 4))),
        "w_value": gaussian(key_list[7], (LAYERS, D, D), D ** -0.5, 0.21875, ((1, 8), (2, 4))),
        "b_value": gaussian(key_list[8], (LAYERS, D), 0.1, 0.6, ((1, 4),), jnp.float32),
        "w_out": gaussian(key_list[9], (LAYERS, D, D), (D // 16) ** -0.5, 0.875, ((1, 8), (2, 4))),
        "b_out": gaussian(key_list[10], (LAYERS, D), 0.5, 3.0, (), jnp.float32),
        "feedforward_norm_gain": jnp.clip(1.0 + 0.18 * jax.random.normal(key_list[11], (LAYERS, D), jnp.float32), 0.1, 1.9),
        "feedforward_norm_bias": gaussian(key_list[12], (LAYERS, D), 0.5, 3.0, (), jnp.float32),
        "w_fc1": gaussian(key_list[13], (LAYERS, D, FF), D ** -0.5, 0.21875, ((1, 8), (2, 4))),
        "b_fc1": gaussian(key_list[14], (LAYERS, FF), 0.5, 3.0, ((1, 4),), jnp.float32),
        "w_fc2": gaussian(key_list[15], (LAYERS, D, FF), FF ** -0.5, 0.109375, ((1, 8), (2, 4))),
        "b_fc2": gaussian(key_list[16], (LAYERS, D), 0.5, 3.0, (), jnp.float32),
    }


EPSILON = 1e-05
HIGH = lax.Precision.HIGHEST

@jax.custom_vjp
def low(v):
    return lax.optimization_barrier(v.astype(jnp.bfloat16)).astype(jnp.float32)

@jax.custom_vjp
def low_back(v):
    return v

def low_keep(v):
    return (low(v), None)

def low_pass(kept, grad):
    return (grad,)

def back_keep(v):
    return (v, None)

def back_low(kept, grad):
    return (low(grad),)
low.defvjp(low_keep, low_pass)
low_back.defvjp(back_keep, back_low)

def matmul_high(left, right):
    return jnp.dot(left, right, precision=HIGH)

def layer_norm(values, norm_gain, shift):
    center = values - lax.optimization_barrier(jnp.mean(values, -1, keepdims=True))
    variance = lax.optimization_barrier(jnp.mean(center * center, -1, keepdims=True))
    return center * lax.rsqrt(variance + EPSILON) * norm_gain + shift

def group_total(left, right):
    frames = left.shape[0]
    parts = jnp.einsum('fgj,dgj->gfd', left.reshape(frames, N_TENSOR, -1), right.reshape(D, N_TENSOR, -1), precision=HIGH)
    return lax.optimization_barrier(jnp.sum(low(parts), 0))

def one_layer(hidden_state, params):
    gain_one, shift_one, w_q, b_q, w_k, w_v, b_v, w_o, b_o, gain_two, shift_two, w_up, b_up, w_down, b_down = params
    frames = hidden_state.shape[0]
    normalized_input = low(layer_norm(hidden_state, gain_one, shift_one))
    queries = low_back(low(matmul_high(normalized_input, w_q) + b_q)).reshape(frames, HEADS, HEAD_DIM)
    keys = low_back(low(matmul_high(normalized_input, w_k))).reshape(frames, HEADS, HEAD_DIM)
    values = low_back(low(matmul_high(normalized_input, w_v) + b_v)).reshape(frames, HEADS, HEAD_DIM)
    scores = low_back(jnp.einsum('qhd,khd->hqk', queries, keys, precision=HIGH) * HEAD_DIM ** (-0.5))
    prob = jax.nn.softmax(scores, axis=-1)
    attended = jnp.einsum('hqk,khd->qhd', low(prob), values, precision=HIGH).reshape(frames, D)
    attended = low_back(low(attended))
    attn_branch = low_back(group_total(attended, w_o) + b_o)
    middle_state = hidden_state + attn_branch
    second_normalized = low(layer_norm(middle_state, gain_two, shift_two))
    pre_act = low_back(matmul_high(second_normalized, w_up) + b_up)
    activated = low(jax.nn.gelu(pre_act, approximate=False))
    mlp_branch = low_back(group_total(activated, w_down) + b_down)
    return middle_state + mlp_branch

def forward(state_all, params):

    def clip_pass(hidden_state):
        for layer_params in range(LAYERS):
            hidden_state = one_layer(hidden_state, tuple((item[layer_params] for item in params)))
        return hidden_state
    return lax.map(jax.checkpoint(clip_pass), state_all)

def reference(inputs, cotangent, attention_norm_gain, attention_norm_bias, w_query, b_query, w_key, w_value, b_value, w_out, b_out, feedforward_norm_gain, feedforward_norm_bias, w_fc1, b_fc1, w_fc2, b_fc2):
    params = (attention_norm_gain, attention_norm_bias, w_query, b_query, w_key, w_value, b_value, w_out, b_out, feedforward_norm_gain, feedforward_norm_bias, w_fc1, b_fc1, w_fc2, b_fc2)
    params = tuple((item.astype(jnp.float32) for item in params))
    encoded, pullback = jax.vjp(forward, inputs.astype(jnp.float32), params)
    state_gradient, grads = pullback(cotangent.astype(jnp.float32))
    return (encoded, state_gradient, grads[0], grads[1], grads[2], grads[3], grads[4], grads[5], grads[6], grads[7], grads[8], grads[9], grads[10], grads[11], grads[12], grads[13], grads[14])
```

```python
import functools
import math

import jax
import jax.numpy as jnp
from jax import lax
from jax.experimental import pallas as pl
from jax.experimental.pallas import tpu as pltpu
from jax.sharding import PartitionSpec as P

HEAD_DIM = 64


EPSILON = 1e-05
INV_ROOT_TWO = 1.0 / math.sqrt(2.0)
INV_ROOT_TWO_PI = 1.0 / math.sqrt(2.0 * math.pi)


def standardize_rows(values):
    center = values - jnp.mean(values, -1, keepdims=True)
    inverse_scale = lax.rsqrt(jnp.mean(center * center, -1, keepdims=True) + EPSILON)
    return (center * inverse_scale, inverse_scale)


def norm_backward_pass(output_gradient, centered_normalized, inverse_scale, norm_gain):
    scaled_values = output_gradient * norm_gain
    return inverse_scale * (
        scaled_values
        - jnp.mean(scaled_values, -1, keepdims=True)
        - centered_normalized * jnp.mean(scaled_values * centered_normalized, -1, keepdims=True)
    )


def times_trans(left, right):
    return lax.dot_general(
        left, right, (((1,), (1,)), ((), ())), preferred_element_type=jnp.float32
    )


def trans_times(left, right):
    return lax.dot_general(
        left, right, (((0,), (0,)), ((), ())), preferred_element_type=jnp.float32
    )


def matmul(left, right):
    return jnp.dot(left, right, preferred_element_type=jnp.float32)


def gelu_slope(pre_act):
    return (
        0.5 * (1.0 + jax.scipy.special.erf(pre_act * INV_ROOT_TWO))
        + pre_act * jnp.exp(-0.5 * pre_act * pre_act) * INV_ROOT_TWO_PI
    )


def split_heads(block):
    return block.reshape(block.shape[0], block.shape[1] // HEAD_DIM, HEAD_DIM)


def attend_forward(query_blk, key_blk, value_blk):
    scale = HEAD_DIM ** (-0.5)
    scores = (
        jnp.einsum(
            "qhd,khd->hqk",
            split_heads(query_blk),
            split_heads(key_blk),
            preferred_element_type=jnp.float32,
        )
        * scale
    )
    top = jnp.max(scores, -1, keepdims=True)
    expo = jnp.exp(scores - top)
    total = jnp.sum(expo, -1, keepdims=True)
    prob = (expo / total).astype(jnp.bfloat16)
    attended = jnp.einsum(
        "hqk,khd->qhd", prob, split_heads(value_blk), preferred_element_type=jnp.float32
    )
    attended = attended.reshape(query_blk.shape[0], -1).astype(jnp.bfloat16)
    return (attended, (top + jnp.log(total))[..., 0])


def score_grads(query_heads, key_heads, value_heads, log_total, grad_heads, inner):
    scale = HEAD_DIM ** (-0.5)
    scores = (
        jnp.einsum("qhd,khd->hqk", query_heads, key_heads, preferred_element_type=jnp.float32)
        * scale
    )
    prob = jnp.exp(scores - log_total[..., None])
    grad_prob = jnp.einsum(
        "qhd,khd->hqk", grad_heads, value_heads, preferred_element_type=jnp.float32
    )
    inner = jnp.sum(prob * grad_prob, -1)
    grad_scores = (prob * (grad_prob - inner[..., None])).astype(jnp.bfloat16)
    return (prob, grad_scores, inner)


def key_side(grad_scores, prob, query_heads, grad_heads, frames_all):
    scale = HEAD_DIM ** (-0.5)
    grad_key = (
        jnp.einsum("hqk,qhd->khd", grad_scores, query_heads, preferred_element_type=jnp.float32)
        * scale
    )
    grad_value = jnp.einsum(
        "hqk,qhd->khd", prob.astype(jnp.bfloat16), grad_heads, preferred_element_type=jnp.float32
    )
    return jnp.concatenate(
        [grad_key.reshape(frames_all, -1), grad_value.reshape(frames_all, -1)], 1
    )


def attend_backward(query_blk, key_blk, value_blk, log_total, grad_blk):
    query_heads = split_heads(query_blk)
    key_heads = split_heads(key_blk)
    grad_heads = split_heads(grad_blk)
    prob, grad_scores, inner = score_grads(
        query_heads, key_heads, split_heads(value_blk), log_total, grad_heads, None
    )
    grad_query = jnp.einsum(
        "hqk,khd->qhd", grad_scores, key_heads, preferred_element_type=jnp.float32
    ) * HEAD_DIM ** (-0.5)
    joined = key_side(grad_scores, prob, query_heads, grad_heads, key_blk.shape[0])
    return (grad_query.reshape(query_blk.shape[0], -1), joined)


MESH = pl.DeviceIdType.MESH
PIECES = 4


def tensor_sum_kernel(part_ref, out_ref, got_pair, mid, got_far, tot, got_back, *sems):
    send_a, recv_a, send_b, recv_b, send_c, recv_c = sems
    me = lax.axis_index("tensor")
    core = lax.rem(me, 2)
    pair = me + 1 - 2 * core
    far = lax.rem(me + 2, 4)
    barrier = pltpu.get_barrier_semaphore()
    for other in (pair, far):
        pl.semaphore_signal(barrier, inc=1, device_id={"tensor": other}, device_id_type=MESH)
    pl.semaphore_wait(barrier, 2)
    half = part_ref.shape[0] // 2
    step = half // PIECES
    mine = core * half
    theirs = (1 - core) * half

    def spot(base, piece):
        return pl.ds(pl.multiple_of(base + piece * step, step), step)

    def here(piece):
        return pl.ds(piece * step, step)

    firsts, seconds, thirds = [], [], []
    for piece in range(PIECES):
        copy = pltpu.make_async_remote_copy(
            src_ref=part_ref.at[spot(theirs, piece)],
            dst_ref=got_pair.at[here(piece)],
            send_sem=send_a.at[piece],
            recv_sem=recv_a.at[piece],
            device_id={"tensor": pair},
            device_id_type=MESH,
        )
        copy.start()
        firsts.append(copy)
    for piece in range(PIECES):
        firsts[piece].wait_recv()
        mid[here(piece)] = (
            part_ref[spot(mine, piece)].astype(jnp.float32)
            + got_pair[here(piece)].astype(jnp.float32)
        ).astype(jnp.bfloat16)
        copy = pltpu.make_async_remote_copy(
            src_ref=mid.at[here(piece)],
            dst_ref=got_far.at[here(piece)],
            send_sem=send_b.at[piece],
            recv_sem=recv_b.at[piece],
            device_id={"tensor": far},
            device_id_type=MESH,
        )
        copy.start()
        seconds.append(copy)
    for piece in range(PIECES):
        seconds[piece].wait_recv()
        total = mid[here(piece)].astype(jnp.float32) + got_far[here(piece)].astype(jnp.float32)
        tot[here(piece)] = total
        out_ref[spot(mine, piece)] = total
        copy = pltpu.make_async_remote_copy(
            src_ref=tot.at[here(piece)],
            dst_ref=got_back.at[here(piece)],
            send_sem=send_c.at[piece],
            recv_sem=recv_c.at[piece],
            device_id={"tensor": pair},
            device_id_type=MESH,
        )
        copy.start()
        thirds.append(copy)
    for piece in range(PIECES):
        thirds[piece].wait_recv()
        out_ref[spot(theirs, piece)] = got_back[here(piece)]
    for copy in firsts + seconds + thirds:
        copy.wait_send()


def tensor_sum(partial_value):
    rows, width = partial_value.shape
    half = rows // 2
    return pl.pallas_call(
        tensor_sum_kernel,
        out_shape=jax.ShapeDtypeStruct((rows, width), jnp.float32),
        in_specs=[pl.BlockSpec(memory_space=pltpu.VMEM)],
        out_specs=pl.BlockSpec(memory_space=pltpu.VMEM),
        scratch_shapes=[
            pltpu.VMEM((half, width), jnp.bfloat16),
            pltpu.VMEM((half, width), jnp.bfloat16),
            pltpu.VMEM((half, width), jnp.bfloat16),
            pltpu.VMEM((half, width), jnp.float32),
            pltpu.VMEM((half, width), jnp.float32),
        ]
        + [pltpu.SemaphoreType.DMA((PIECES,))] * 6,
        compiler_params=pltpu.CompilerParams(
            collective_id=0, has_side_effects=True, vmem_limit_bytes=16 * 2**20
        ),
        cost_estimate=pl.CostEstimate(
            flops=rows * width * 4, bytes_accessed=20_000_000, transcendentals=0
        ),
        name="tensor_sum",
    )(partial_value.astype(jnp.bfloat16))


def small_sum_kernel(count, dp_count, part_ref, out_ref, slots, own_sem, send_sem, recv_sem):
    me = lax.axis_index("seq") * dp_count + lax.axis_index("dp")

    def place(shift):
        other = lax.rem(me + shift, count)
        return {"seq": other // dp_count, "dp": lax.rem(other, dp_count)}

    barrier = pltpu.get_barrier_semaphore()
    for shift in range(1, count):
        pl.semaphore_signal(barrier, inc=1, device_id=place(shift), device_id_type=MESH)
    pl.semaphore_wait(barrier, count - 1)
    copies = []
    for shift in range(1, count):
        copy = pltpu.make_async_remote_copy(
            src_ref=part_ref,
            dst_ref=slots.at[me],
            send_sem=send_sem.at[shift],
            recv_sem=recv_sem.at[shift],
            device_id=place(shift),
            device_id_type=MESH,
        )
        copy.start()
        copies.append(copy)
    own = pltpu.make_async_copy(part_ref, slots.at[me], own_sem)
    own.start()
    own.wait()
    for copy in copies:
        copy.wait()
    total = slots[0]
    for index in range(1, count):
        total = total + slots[index]
    out_ref[...] = total


def small_sum(packed):
    count = lax.axis_size(("seq", "dp"))
    dp_count = lax.axis_size("dp")
    return pl.pallas_call(
        functools.partial(small_sum_kernel, count, dp_count),
        out_shape=jax.ShapeDtypeStruct(packed.shape, jnp.float32),
        in_specs=[pl.BlockSpec(memory_space=pltpu.VMEM)],
        out_specs=pl.BlockSpec(memory_space=pltpu.VMEM),
        scratch_shapes=[
            pltpu.VMEM((count,) + packed.shape, jnp.float32),
            pltpu.SemaphoreType.DMA,
            pltpu.SemaphoreType.DMA((count,)),
            pltpu.SemaphoreType.DMA((count,)),
        ],
        compiler_params=pltpu.CompilerParams(
            collective_id=1, has_side_effects=True, vmem_limit_bytes=16 * 2**20
        ),
        cost_estimate=pl.CostEstimate(flops=1000, bytes_accessed=20_000_000, transcendentals=0),
        name="small_sum",
    )(packed)


def per_device(
    inputs,
    cotangent,
    attention_norm_gain,
    attention_norm_bias,
    w_query,
    b_query,
    w_key,
    w_value,
    b_value,
    w_out,
    b_out,
    feedforward_norm_gain,
    feedforward_norm_bias,
    w_fc1,
    b_fc1,
    w_fc2,
    b_fc2,
):
    clips, frames_local, width = inputs.shape
    rows = clips * frames_local
    layers = w_query.shape[0]
    cols = w_query.shape[2]
    hidden = w_fc1.shape[2]
    group = ("seq", "dp")
    hidden_state = inputs.astype(jnp.float32).reshape(rows, width)
    full_first, full_rest = [], []
    for layer in range(layers):
        first = jnp.concatenate([w_query[layer], w_key[layer], w_value[layer]], 1)
        rest = jnp.concatenate([w_fc1[layer], w_fc2[layer], w_out[layer]], 1)
        full_first.append(lax.all_gather(first, group, axis=0, tiled=True))
        full_rest.append(lax.all_gather(rest, group, axis=0, tiled=True))
    saved_all = []
    for layer in range(layers):
        full_qkv = full_first[layer]
        full_up = full_rest[layer][:, :hidden]
        full_down = full_rest[layer][:, hidden : 2 * hidden]
        full_o = full_rest[layer][:, 2 * hidden :]
        xhat1, rstd1 = standardize_rows(hidden_state)
        normed1 = (xhat1 * attention_norm_gain[layer] + attention_norm_bias[layer]).astype(
            jnp.bfloat16
        )
        bias = jnp.concatenate([b_query[layer], jnp.zeros_like(b_query[layer]), b_value[layer]])
        qkv = (matmul(normed1, full_qkv) + bias).astype(jnp.bfloat16)
        queries = qkv[:, :cols].reshape(clips, frames_local, cols)
        kv_local = qkv[:, cols:].reshape(clips, frames_local, 2 * cols)
        kv_all = lax.all_gather(kv_local, "seq", axis=1, tiled=True)
        outcomes = [
            attend_forward(queries[clip], kv_all[clip, :, :cols], kv_all[clip, :, cols:])
            for clip in range(clips)
        ]
        log_total = [outcome[1] for outcome in outcomes]
        attended = jnp.concatenate([outcome[0] for outcome in outcomes], 0)
        middle_state = hidden_state + (tensor_sum(times_trans(attended, full_o)) + b_out[layer])
        xhat2, rstd2 = standardize_rows(middle_state)
        normed2 = (xhat2 * feedforward_norm_gain[layer] + feedforward_norm_bias[layer]).astype(
            jnp.bfloat16
        )
        pre_act = matmul(normed2, full_up) + b_fc1[layer]
        activated = jax.nn.gelu(pre_act, approximate=False).astype(jnp.bfloat16)
        hidden_state = middle_state + (
            tensor_sum(times_trans(activated, full_down)) + b_fc2[layer]
        )
        saved_all.append(
            (xhat1, rstd1, normed1, queries, kv_all, log_total, attended, xhat2, rstd2, normed2, pre_act, activated)
        )
    encoded = hidden_state.reshape(clips, frames_local, width)
    state_gradient = cotangent.reshape(rows, width)
    grads_first, grads_rest, smalls = [None] * layers, [None] * layers, [None] * layers
    for layer in reversed(range(layers)):
        full_qkv = full_first[layer]
        full_up = full_rest[layer][:, :hidden]
        full_down = full_rest[layer][:, hidden : 2 * hidden]
        full_o = full_rest[layer][:, 2 * hidden :]
        (xhat1, rstd1, normed1, queries, kv_all, log_total, attended, xhat2, rstd2, normed2, pre_act, activated) = saved_all[layer]
        grad_mlp = state_gradient.astype(jnp.bfloat16)
        grad_pre = (matmul(grad_mlp, full_down) * gelu_slope(pre_act)).astype(jnp.bfloat16)
        grad_norm2 = tensor_sum(times_trans(grad_pre, full_up))
        middle_gradient = state_gradient + norm_backward_pass(
            grad_norm2, xhat2, rstd2, feedforward_norm_gain[layer]
        )
        grad_attn = middle_gradient.astype(jnp.bfloat16)
        rest_terms = jnp.concatenate(
            [
                trans_times(normed2, grad_pre).astype(jnp.bfloat16),
                trans_times(grad_mlp, activated).astype(jnp.bfloat16),
                trans_times(grad_attn, attended).astype(jnp.bfloat16),
            ],
            1,
        )
        grads_rest[layer] = lax.psum_scatter(rest_terms, group, scatter_dimension=0, tiled=True)
        grad_attended = (
            matmul(grad_attn, full_o).astype(jnp.bfloat16).reshape(clips, frames_local, cols)
        )
        outcomes = [
            attend_backward(
                queries[clip],
                kv_all[clip, :, :cols],
                kv_all[clip, :, cols:],
                log_total[clip],
                grad_attended[clip],
            )
            for clip in range(clips)
        ]
        kv_terms = jnp.stack([outcome[1] for outcome in outcomes], 0).astype(jnp.bfloat16)
        kv_grads = lax.psum_scatter(kv_terms, "seq", scatter_dimension=1, tiled=True)
        grad_query = jnp.concatenate([outcome[0] for outcome in outcomes], 0).astype(jnp.bfloat16)
        grad_qkv = jnp.concatenate([grad_query, kv_grads.reshape(rows, 2 * cols)], 1)
        grads_first[layer] = lax.psum_scatter(
            trans_times(normed1, grad_qkv).astype(jnp.bfloat16),
            group,
            scatter_dimension=0,
            tiled=True,
        )
        grad_norm1 = tensor_sum(times_trans(grad_qkv, full_qkv))
        state_gradient = middle_gradient + norm_backward_pass(
            grad_norm1, xhat1, rstd1, attention_norm_gain[layer]
        )
        sums_qkv = jnp.sum(grad_qkv, 0, dtype=jnp.float32)
        smalls[layer] = (
            jnp.sum(grad_norm1 * xhat1, 0),
            jnp.sum(grad_norm1, 0),
            sums_qkv[:cols],
            sums_qkv[2 * cols :],
            jnp.sum(grad_attn, 0, dtype=jnp.float32),
            jnp.sum(grad_norm2 * xhat2, 0),
            jnp.sum(grad_norm2, 0),
            jnp.sum(grad_pre, 0, dtype=jnp.float32),
            jnp.sum(grad_mlp, 0, dtype=jnp.float32),
        )
    flat = jnp.concatenate([part for layer in range(layers) for part in smalls[layer]])
    length = flat.shape[0]
    padded = -(-length // 1024) * 1024
    packed = jnp.pad(flat, (0, padded - length)).reshape(padded // 128, 128)
    summed = small_sum(packed).reshape(padded)
    small_stack, offset = [[] for _ in range(9)], 0
    for layer in range(layers):
        for member in range(9):
            size = smalls[layer][member].shape[0]
            small_stack[member].append(summed[offset : offset + size])
            offset += size
    small_stack = [jnp.stack(members, 0) for members in small_stack]
    first_out = [grad.astype(jnp.float32) for grad in grads_first]
    rest_out = [grad.astype(jnp.float32) for grad in grads_rest]

    def pick(parts, start, size):
        return jnp.stack([part[:, start : start + size] for part in parts], 0)

    grad_inputs = state_gradient.reshape(clips, frames_local, width)
    return (
        encoded,
        grad_inputs,
        small_stack[0],
        small_stack[1],
        pick(first_out, 0, cols),
        small_stack[2],
        pick(first_out, cols, cols),
        pick(first_out, 2 * cols, cols),
        small_stack[3],
        pick(rest_out, 2 * hidden, cols),
        small_stack[4],
        small_stack[5],
        small_stack[6],
        pick(rest_out, 0, hidden),
        small_stack[7],
        pick(rest_out, hidden, hidden),
        small_stack[8],
    )


def solution(mesh):
    placed = (
        P("dp", "seq", None),
        P("dp", "seq", None),
        P(),
        P(),
        P(None, ("seq", "dp"), "tensor"),
        P(None, "tensor"),
        P(None, ("seq", "dp"), "tensor"),
        P(None, ("seq", "dp"), "tensor"),
        P(None, "tensor"),
        P(None, ("seq", "dp"), "tensor"),
        P(),
        P(),
        P(),
        P(None, ("seq", "dp"), "tensor"),
        P(None, "tensor"),
        P(None, ("seq", "dp"), "tensor"),
        P(),
    )
    return jax.shard_map(
        per_device,
        mesh=mesh,
        in_specs=placed,
        out_specs=(
            P("dp", "seq", None),
            P("dp", "seq", None),
            P(),
            P(),
            P(None, ("seq", "dp"), "tensor"),
            P(None, "tensor"),
            P(None, ("seq", "dp"), "tensor"),
            P(None, ("seq", "dp"), "tensor"),
            P(None, "tensor"),
            P(None, ("seq", "dp"), "tensor"),
            P(),
            P(),
            P(),
            P(None, ("seq", "dp"), "tensor"),
            P(None, "tensor"),
            P(None, ("seq", "dp"), "tensor"),
            P(),
        ),
        check_vma=False,
    )
```

```python
import functools
import math

import jax
import jax.numpy as jnp
from jax import lax
from jax.experimental import pallas as pl
from jax.experimental.pallas import tpu as pltpu
from jax.sharding import PartitionSpec as P

HEAD_DIM = 64


EPSILON = 1e-05
INV_ROOT_TWO = 1.0 / math.sqrt(2.0)
INV_ROOT_TWO_PI = 1.0 / math.sqrt(2.0 * math.pi)


def standardize_rows(values):
    center = values - jnp.mean(values, -1, keepdims=True)
    inverse_scale = lax.rsqrt(jnp.mean(center * center, -1, keepdims=True) + EPSILON)
    return (center * inverse_scale, inverse_scale)


def norm_backward_pass(output_gradient, centered_normalized, inverse_scale, norm_gain):
    scaled_values = output_gradient * norm_gain
    return inverse_scale * (
        scaled_values
        - jnp.mean(scaled_values, -1, keepdims=True)
        - centered_normalized * jnp.mean(scaled_values * centered_normalized, -1, keepdims=True)
    )


def times_trans(left, right):
    return lax.dot_general(
        left, right, (((1,), (1,)), ((), ())), preferred_element_type=jnp.float32
    )


def trans_times(left, right):
    return lax.dot_general(
        left, right, (((0,), (0,)), ((), ())), preferred_element_type=jnp.float32
    )


def matmul(left, right):
    return jnp.dot(left, right, preferred_element_type=jnp.float32)


def gelu_slope(pre_act):
    return (
        0.5 * (1.0 + jax.scipy.special.erf(pre_act * INV_ROOT_TWO))
        + pre_act * jnp.exp(-0.5 * pre_act * pre_act) * INV_ROOT_TWO_PI
    )


def split_heads(block):
    return block.reshape(block.shape[0], block.shape[1] // HEAD_DIM, HEAD_DIM)


def attend_forward(query_blk, key_blk, value_blk):
    scale = HEAD_DIM ** (-0.5)
    scores = (
        jnp.einsum(
            "qhd,khd->hqk",
            split_heads(query_blk),
            split_heads(key_blk),
            preferred_element_type=jnp.float32,
        )
        * scale
    )
    top = jnp.max(scores, -1, keepdims=True)
    expo = jnp.exp(scores - top)
    total = jnp.sum(expo, -1, keepdims=True)
    prob = (expo / total).astype(jnp.bfloat16)
    attended = jnp.einsum(
        "hqk,khd->qhd", prob, split_heads(value_blk), preferred_element_type=jnp.float32
    )
    attended = attended.reshape(query_blk.shape[0], -1).astype(jnp.bfloat16)
    return (attended, (top + jnp.log(total))[..., 0])


def score_grads(query_heads, key_heads, value_heads, log_total, grad_heads, inner):
    scale = HEAD_DIM ** (-0.5)
    scores = (
        jnp.einsum("qhd,khd->hqk", query_heads, key_heads, preferred_element_type=jnp.float32)
        * scale
    )
    prob = jnp.exp(scores - log_total[..., None])
    grad_prob = jnp.einsum(
        "qhd,khd->hqk", grad_heads, value_heads, preferred_element_type=jnp.float32
    )
    inner = jnp.sum(prob * grad_prob, -1)
    grad_scores = (prob * (grad_prob - inner[..., None])).astype(jnp.bfloat16)
    return (prob, grad_scores, inner)


def key_side(grad_scores, prob, query_heads, grad_heads, frames_all):
    scale = HEAD_DIM ** (-0.5)
    grad_key = (
        jnp.einsum("hqk,qhd->khd", grad_scores, query_heads, preferred_element_type=jnp.float32)
        * scale
    )
    grad_value = jnp.einsum(
        "hqk,qhd->khd", prob.astype(jnp.bfloat16), grad_heads, preferred_element_type=jnp.float32
    )
    return jnp.concatenate(
        [grad_key.reshape(frames_all, -1), grad_value.reshape(frames_all, -1)], 1
    )


def attend_backward(query_blk, key_blk, value_blk, log_total, grad_blk):
    query_heads = split_heads(query_blk)
    key_heads = split_heads(key_blk)
    grad_heads = split_heads(grad_blk)
    prob, grad_scores, inner = score_grads(
        query_heads, key_heads, split_heads(value_blk), log_total, grad_heads, None
    )
    grad_query = jnp.einsum(
        "hqk,khd->qhd", grad_scores, key_heads, preferred_element_type=jnp.float32
    ) * HEAD_DIM ** (-0.5)
    joined = key_side(grad_scores, prob, query_heads, grad_heads, key_blk.shape[0])
    return (grad_query.reshape(query_blk.shape[0], -1), joined)


MESH = pl.DeviceIdType.MESH
PIECES = 4


def tensor_sum_kernel(part_ref, out_ref, got_pair, mid, got_far, tot, got_back, *sems):
    send_a, recv_a, send_b, recv_b, send_c, recv_c = sems
    me = lax.axis_index("tensor")
    core = lax.rem(me, 2)
    pair = me + 1 - 2 * core
    far = lax.rem(me + 2, 4)
    barrier = pltpu.get_barrier_semaphore()
    for other in (pair, far):
        pl.semaphore_signal(barrier, inc=1, device_id={"tensor": other}, device_id_type=MESH)
    pl.semaphore_wait(barrier, 2)
    half = part_ref.shape[0] // 2
    step = half // PIECES
    mine = core * half
    theirs = (1 - core) * half

    def spot(base, piece):
        return pl.ds(pl.multiple_of(base + piece * step, step), step)

    def here(piece):
        return pl.ds(piece * step, step)

    firsts, seconds, thirds = [], [], []
    for piece in range(PIECES):
        copy = pltpu.make_async_remote_copy(
            src_ref=part_ref.at[spot(theirs, piece)],
            dst_ref=got_pair.at[here(piece)],
            send_sem=send_a.at[piece],
            recv_sem=recv_a.at[piece],
            device_id={"tensor": pair},
            device_id_type=MESH,
        )
        copy.start()
        firsts.append(copy)
    for piece in range(PIECES):
        firsts[piece].wait_recv()
        mid[here(piece)] = (
            part_ref[spot(mine, piece)].astype(jnp.float32)
            + got_pair[here(piece)].astype(jnp.float32)
        ).astype(jnp.bfloat16)
        copy = pltpu.make_async_remote_copy(
            src_ref=mid.at[here(piece)],
            dst_ref=got_far.at[here(piece)],
            send_sem=send_b.at[piece],
            recv_sem=recv_b.at[piece],
            device_id={"tensor": far},
            device_id_type=MESH,
        )
        copy.start()
        seconds.append(copy)
    for piece in range(PIECES):
        seconds[piece].wait_recv()
        total = mid[here(piece)].astype(jnp.float32) + got_far[here(piece)].astype(jnp.float32)
        tot[here(piece)] = total
        out_ref[spot(mine, piece)] = total
        copy = pltpu.make_async_remote_copy(
            src_ref=tot.at[here(piece)],
            dst_ref=got_back.at[here(piece)],
            send_sem=send_c.at[piece],
            recv_sem=recv_c.at[piece],
            device_id={"tensor": pair},
            device_id_type=MESH,
        )
        copy.start()
        thirds.append(copy)
    for piece in range(PIECES):
        thirds[piece].wait_recv()
        out_ref[spot(theirs, piece)] = got_back[here(piece)]
    for copy in firsts + seconds + thirds:
        copy.wait_send()


def tensor_sum(partial_value):
    rows, width = partial_value.shape
    half = rows // 2
    return pl.pallas_call(
        tensor_sum_kernel,
        out_shape=jax.ShapeDtypeStruct((rows, width), jnp.float32),
        in_specs=[pl.BlockSpec(memory_space=pltpu.VMEM)],
        out_specs=pl.BlockSpec(memory_space=pltpu.VMEM),
        scratch_shapes=[
            pltpu.VMEM((half, width), jnp.bfloat16),
            pltpu.VMEM((half, width), jnp.bfloat16),
            pltpu.VMEM((half, width), jnp.bfloat16),
            pltpu.VMEM((half, width), jnp.float32),
            pltpu.VMEM((half, width), jnp.float32),
        ]
        + [pltpu.SemaphoreType.DMA((PIECES,))] * 6,
        compiler_params=pltpu.CompilerParams(
            collective_id=0, has_side_effects=True, vmem_limit_bytes=16 * 2**20
        ),
        cost_estimate=pl.CostEstimate(
            flops=rows * width * 4, bytes_accessed=20_000_000, transcendentals=0
        ),
        name="tensor_sum",
    )(partial_value.astype(jnp.bfloat16))


def gather_kernel(seqs, dps, forward, own_ref, out_ref, own_sem, send_z, recv_z, *sems):
    s, d = lax.axis_index("seq"), lax.axis_index("dp")

    def along(k):
        return {"seq": lax.rem(s + k, seqs)}

    def across(j):
        return {"dp": lax.rem(d + j, dps)}

    def slot(k):
        source = lax.rem(s + seqs - k, seqs)
        return source * dps + d if forward else source

    barrier = pltpu.get_barrier_semaphore()
    others = [along(k) for k in range(1, seqs)]
    if forward:
        others += [across(j) for j in range(1, dps)]
    for other in others:
        pl.semaphore_signal(barrier, inc=1, device_id=other, device_id_type=MESH)
    pl.semaphore_wait(barrier, len(others))
    firsts, seconds = [], []
    for k in range(1, seqs):
        copy = pltpu.make_async_remote_copy(
            src_ref=own_ref,
            dst_ref=out_ref.at[slot(0)],
            send_sem=send_z.at[k],
            recv_sem=recv_z.at[k],
            device_id=along(k),
            device_id_type=MESH,
        )
        copy.start()
        firsts.append(copy)
    own = pltpu.make_async_copy(own_ref, out_ref.at[slot(0)], own_sem)
    own.start()
    for k in (0, 1, seqs - 1) + tuple(range(2, seqs - 1)):
        if k:
            firsts[k - 1].wait_recv()
        if forward:
            send_y, recv_y = sems
            for j in range(1, dps):
                copy = pltpu.make_async_remote_copy(
                    src_ref=out_ref.at[slot(k)] if k else own_ref,
                    dst_ref=out_ref.at[slot(k)],
                    send_sem=send_y.at[k * dps + j],
                    recv_sem=recv_y.at[k * dps + j],
                    device_id=across(j),
                    device_id_type=MESH,
                )
                copy.start()
                seconds.append(copy)
    own.wait()
    for copy in firsts:
        copy.wait_send()
    for copy in seconds:
        copy.wait()


def gather_slots(block, forward):
    seqs, dps = lax.axis_size("seq"), lax.axis_size("dp")
    count = seqs * dps if forward else seqs
    sems = [pltpu.SemaphoreType.DMA((seqs,))] * 2
    if forward:
        sems += [pltpu.SemaphoreType.DMA((seqs * dps,))] * 2
    return pl.pallas_call(
        functools.partial(gather_kernel, seqs, dps, forward),
        out_shape=jax.ShapeDtypeStruct((count,) + block.shape, block.dtype),
        in_specs=[pl.BlockSpec(memory_space=pl.ANY)],
        out_specs=pl.BlockSpec(memory_space=pl.ANY),
        scratch_shapes=[pltpu.SemaphoreType.DMA] + sems,
        compiler_params=pltpu.CompilerParams(
            collective_id=2 if forward else 3, has_side_effects=True, vmem_limit_bytes=16 * 2**20
        ),
        cost_estimate=pl.CostEstimate(
            flops=1000, bytes_accessed=100_000_000 if forward else 40_000_000, transcendentals=0
        ),
        name="gather_weights" if forward else "gather_frames",
    )(block)


def frame_sum_kernel(seqs, part_ref, out_ref, got, send_sem, recv_sem):
    s = lax.axis_index("seq")
    barrier = pltpu.get_barrier_semaphore()
    for k in range(1, seqs):
        pl.semaphore_signal(
            barrier, inc=1, device_id={"seq": lax.rem(s + k, seqs)}, device_id_type=MESH
        )
    pl.semaphore_wait(barrier, seqs - 1)
    copies = []
    for k in range(1, seqs):
        other = lax.rem(s + k, seqs)
        copy = pltpu.make_async_remote_copy(
            src_ref=part_ref.at[other],
            dst_ref=got.at[k],
            send_sem=send_sem.at[k],
            recv_sem=recv_sem.at[k],
            device_id={"seq": other},
            device_id_type=MESH,
        )
        copy.start()
        copies.append(copy)
    for copy in copies:
        copy.wait_recv()
    total = part_ref[s].astype(jnp.float32)
    for k in range(1, seqs):
        total = total + got[k].astype(jnp.float32)
    out_ref[...] = total.astype(jnp.bfloat16)
    for copy in copies:
        copy.wait_send()


def frame_sum(parts):
    seqs = lax.axis_size("seq")
    return pl.pallas_call(
        functools.partial(frame_sum_kernel, seqs),
        out_shape=jax.ShapeDtypeStruct(parts.shape[1:], jnp.bfloat16),
        in_specs=[pl.BlockSpec(memory_space=pltpu.VMEM)],
        out_specs=pl.BlockSpec(memory_space=pltpu.VMEM),
        scratch_shapes=[
            pltpu.VMEM(parts.shape, jnp.bfloat16),
            pltpu.SemaphoreType.DMA((seqs,)),
            pltpu.SemaphoreType.DMA((seqs,)),
        ],
        compiler_params=pltpu.CompilerParams(
            collective_id=4, has_side_effects=True, vmem_limit_bytes=16 * 2**20
        ),
        cost_estimate=pl.CostEstimate(flops=1000, bytes_accessed=40_000_000, transcendentals=0),
        name="frame_sum",
    )(parts)


def grad_sum_kernel(
    seqs, dps, part_ref, small_ref, out_ref, small_out, got_y, mid, got_z, slots,
    own_sem, send_s, recv_s, send_y, recv_y, send_z, recv_z,
):
    s, d = lax.axis_index("seq"), lax.axis_index("dp")
    count = seqs * dps
    me = s * dps + d

    def place(shift):
        other = lax.rem(me + shift, count)
        return {"seq": other // dps, "dp": lax.rem(other, dps)}

    barrier = pltpu.get_barrier_semaphore()
    for shift in range(1, count):
        pl.semaphore_signal(barrier, inc=1, device_id=place(shift), device_id_type=MESH)
    pl.semaphore_wait(barrier, count - 1)
    order = tuple(range(1, seqs)) + (0,)
    firsts, seconds, smalls = {}, {}, []
    for k in order:
        for j in range(1, dps):
            to = lax.rem(d + j, dps)
            copy = pltpu.make_async_remote_copy(
                src_ref=part_ref.at[lax.rem(s + k, seqs) * dps + to],
                dst_ref=got_y.at[k * dps + j],
                send_sem=send_y.at[k * dps + j],
                recv_sem=recv_y.at[k * dps + j],
                device_id={"dp": to},
                device_id_type=MESH,
            )
            copy.start()
            firsts[k, j] = copy
    for shift in range(1, count):
        copy = pltpu.make_async_remote_copy(
            src_ref=small_ref,
            dst_ref=slots.at[me],
            send_sem=send_s.at[shift],
            recv_sem=recv_s.at[shift],
            device_id=place(shift),
            device_id_type=MESH,
        )
        copy.start()
        smalls.append(copy)
    own = pltpu.make_async_copy(small_ref, slots.at[me], own_sem)
    own.start()
    for k in order:
        total = part_ref[lax.rem(s + k, seqs) * dps + d].astype(jnp.float32)
        for j in range(1, dps):
            firsts[k, j].wait_recv()
            total = total + got_y[k * dps + j].astype(jnp.float32)
        if k:
            mid[k] = total.astype(jnp.bfloat16)
            copy = pltpu.make_async_remote_copy(
                src_ref=mid.at[k],
                dst_ref=got_z.at[k],
                send_sem=send_z.at[k],
                recv_sem=recv_z.at[k],
                device_id={"seq": lax.rem(s + k, seqs)},
                device_id_type=MESH,
            )
            copy.start()
            seconds[k] = copy
        else:
            out_ref[...] = total
    own.wait()
    for copy in smalls:
        copy.wait()
    total = slots[0]
    for index in range(1, count):
        total = total + slots[index]
    small_out[...] = total
    for k in range(1, seqs):
        seconds[k].wait_recv()
        out_ref[...] = out_ref[...] + got_z[k].astype(jnp.float32)
    for copy in firsts.values():
        copy.wait_send()
    for copy in seconds.values():
        copy.wait_send()


def grad_sum(parts, packed):
    seqs, dps = lax.axis_size("seq"), lax.axis_size("dp")
    count = seqs * dps
    block = parts.shape[1:]
    vmem = pl.BlockSpec(memory_space=pltpu.VMEM)
    return pl.pallas_call(
        functools.partial(grad_sum_kernel, seqs, dps),
        out_shape=(
            jax.ShapeDtypeStruct(block, jnp.float32),
            jax.ShapeDtypeStruct(packed.shape, jnp.float32),
        ),
        in_specs=[vmem, vmem],
        out_specs=(vmem, vmem),
        scratch_shapes=[
            pltpu.VMEM((count,) + block, jnp.bfloat16),
            pltpu.VMEM((seqs,) + block, jnp.bfloat16),
            pltpu.VMEM((seqs,) + block, jnp.bfloat16),
            pltpu.VMEM((count,) + packed.shape, jnp.float32),
            pltpu.SemaphoreType.DMA,
            pltpu.SemaphoreType.DMA((count,)),
            pltpu.SemaphoreType.DMA((count,)),
            pltpu.SemaphoreType.DMA((count,)),
            pltpu.SemaphoreType.DMA((count,)),
            pltpu.SemaphoreType.DMA((seqs,)),
            pltpu.SemaphoreType.DMA((seqs,)),
        ],
        compiler_params=pltpu.CompilerParams(
            collective_id=1, has_side_effects=True, vmem_limit_bytes=32 * 2**20
        ),
        cost_estimate=pl.CostEstimate(flops=1000, bytes_accessed=100_000_000, transcendentals=0),
        name="grad_sum",
    )(parts, packed)


def per_device(
    inputs,
    cotangent,
    attention_norm_gain,
    attention_norm_bias,
    w_query,
    b_query,
    w_key,
    w_value,
    b_value,
    w_out,
    b_out,
    feedforward_norm_gain,
    feedforward_norm_bias,
    w_fc1,
    b_fc1,
    w_fc2,
    b_fc2,
):
    clips, frames_local, width = inputs.shape
    rows = clips * frames_local
    layers = w_query.shape[0]
    cols = w_query.shape[2]
    hidden = w_fc1.shape[2]
    group = ("seq", "dp")
    hidden_state = inputs.astype(jnp.float32).reshape(rows, width)
    full_first, full_rest = [], []
    for layer in range(layers):
        joined = jnp.concatenate(
            [
                w_fc1[layer],
                w_fc2[layer],
                w_query[layer],
                w_key[layer],
                w_value[layer],
                w_out[layer],
            ],
            1,
        )
        if layer == 0:
            whole = gather_slots(joined, True).reshape(width, joined.shape[1])
        else:
            whole = lax.all_gather(joined, group, axis=0, tiled=True)
        full_first.append(whole[:, 2 * hidden : 2 * hidden + 3 * cols])
        full_rest.append((whole[:, :hidden], whole[:, hidden : 2 * hidden], whole[:, 2 * hidden + 3 * cols :]))
    saved_all = []
    for layer in range(layers):
        full_qkv = full_first[layer]
        full_up, full_down, full_o = full_rest[layer]
        xhat1, rstd1 = standardize_rows(hidden_state)
        normed1 = (xhat1 * attention_norm_gain[layer] + attention_norm_bias[layer]).astype(
            jnp.bfloat16
        )
        bias = jnp.concatenate([b_query[layer], jnp.zeros_like(b_query[layer]), b_value[layer]])
        qkv = (matmul(normed1, full_qkv) + bias).astype(jnp.bfloat16)
        queries = qkv[:, :cols].reshape(clips, frames_local, cols)
        kv_all = (
            gather_slots(qkv[:, cols:], False)
            .reshape(-1, clips, frames_local, 2 * cols)
            .transpose(1, 0, 2, 3)
            .reshape(clips, -1, 2 * cols)
        )
        outcomes = [
            attend_forward(queries[clip], kv_all[clip, :, :cols], kv_all[clip, :, cols:])
            for clip in range(clips)
        ]
        log_total = [outcome[1] for outcome in outcomes]
        attended = jnp.concatenate([outcome[0] for outcome in outcomes], 0)
        middle_state = hidden_state + (tensor_sum(times_trans(attended, full_o)) + b_out[layer])
        xhat2, rstd2 = standardize_rows(middle_state)
        normed2 = (xhat2 * feedforward_norm_gain[layer] + feedforward_norm_bias[layer]).astype(
            jnp.bfloat16
        )
        pre_act = matmul(normed2, full_up) + b_fc1[layer]
        activated = jax.nn.gelu(pre_act, approximate=False).astype(jnp.bfloat16)
        hidden_state = middle_state + (
            tensor_sum(times_trans(activated, full_down)) + b_fc2[layer]
        )
        saved_all.append(
            (xhat1, rstd1, normed1, queries, kv_all, log_total, attended, xhat2, rstd2, normed2, pre_act, activated)
        )
    encoded = hidden_state.reshape(clips, frames_local, width)
    state_gradient = cotangent.reshape(rows, width)
    big_grads, smalls = [None] * layers, [None] * layers
    for layer in reversed(range(layers)):
        full_qkv = full_first[layer]
        full_up, full_down, full_o = full_rest[layer]
        (xhat1, rstd1, normed1, queries, kv_all, log_total, attended, xhat2, rstd2, normed2, pre_act, activated) = saved_all[layer]
        grad_mlp = state_gradient.astype(jnp.bfloat16)
        grad_pre = (matmul(grad_mlp, full_down) * gelu_slope(pre_act)).astype(jnp.bfloat16)
        grad_norm2 = tensor_sum(times_trans(grad_pre, full_up))
        middle_gradient = state_gradient + norm_backward_pass(
            grad_norm2, xhat2, rstd2, feedforward_norm_gain[layer]
        )
        grad_attn = middle_gradient.astype(jnp.bfloat16)
        grad_attended = (
            matmul(grad_attn, full_o).astype(jnp.bfloat16).reshape(clips, frames_local, cols)
        )
        outcomes = [
            attend_backward(
                queries[clip],
                kv_all[clip, :, :cols],
                kv_all[clip, :, cols:],
                log_total[clip],
                grad_attended[clip],
            )
            for clip in range(clips)
        ]
        kv_terms = jnp.stack([outcome[1] for outcome in outcomes], 0).astype(jnp.bfloat16)
        kv_grads = frame_sum(
            kv_terms.reshape(clips, -1, frames_local, 2 * cols)
            .transpose(1, 0, 2, 3)
            .reshape(-1, rows, 2 * cols)
        )
        grad_query = jnp.concatenate([outcome[0] for outcome in outcomes], 0).astype(jnp.bfloat16)
        grad_qkv = jnp.concatenate([grad_query, kv_grads], 1)
        all_terms = jnp.concatenate(
            [
                trans_times(normed2, grad_pre).astype(jnp.bfloat16),
                trans_times(grad_mlp, activated).astype(jnp.bfloat16),
                trans_times(normed1, grad_qkv).astype(jnp.bfloat16),
                trans_times(grad_attn, attended).astype(jnp.bfloat16),
            ],
            1,
        )
        if layer:
            big_grads[layer] = lax.psum_scatter(
                all_terms, group, scatter_dimension=0, tiled=True
            ).astype(jnp.float32)
        grad_norm1 = tensor_sum(times_trans(grad_qkv, full_qkv))
        state_gradient = middle_gradient + norm_backward_pass(
            grad_norm1, xhat1, rstd1, attention_norm_gain[layer]
        )
        sums_qkv = jnp.sum(grad_qkv, 0, dtype=jnp.float32)
        smalls[layer] = (
            jnp.sum(grad_norm1 * xhat1, 0),
            jnp.sum(grad_norm1, 0),
            sums_qkv[:cols],
            sums_qkv[2 * cols :],
            jnp.sum(grad_attn, 0, dtype=jnp.float32),
            jnp.sum(grad_norm2 * xhat2, 0),
            jnp.sum(grad_norm2, 0),
            jnp.sum(grad_pre, 0, dtype=jnp.float32),
            jnp.sum(grad_mlp, 0, dtype=jnp.float32),
        )
    flat = jnp.concatenate([part for layer in range(layers) for part in smalls[layer]])
    length = flat.shape[0]
    padded = -(-length // 1024) * 1024
    packed = jnp.pad(flat, (0, padded - length)).reshape(padded // 128, 128)
    parts = all_terms.reshape(lax.axis_size(group), -1, all_terms.shape[1])
    big_grads[0], summed = grad_sum(parts, packed)
    summed = summed.reshape(padded)
    small_stack, offset = [[] for _ in range(9)], 0
    for layer in range(layers):
        for member in range(9):
            size = smalls[layer][member].shape[0]
            small_stack[member].append(summed[offset : offset + size])
            offset += size
    small_stack = [jnp.stack(members, 0) for members in small_stack]

    def pick(start, size):
        return jnp.stack([part[:, start : start + size] for part in big_grads], 0)

    grad_inputs = state_gradient.reshape(clips, frames_local, width)
    return (
        encoded,
        grad_inputs,
        small_stack[0],
        small_stack[1],
        pick(2 * hidden, cols),
        small_stack[2],
        pick(2 * hidden + cols, cols),
        pick(2 * hidden + 2 * cols, cols),
        small_stack[3],
        pick(2 * hidden + 3 * cols, cols),
        small_stack[4],
        small_stack[5],
        small_stack[6],
        pick(0, hidden),
        small_stack[7],
        pick(hidden, hidden),
        small_stack[8],
    )


def solution(mesh):
    placed = (
        P("dp", "seq", None),
        P("dp", "seq", None),
        P(),
        P(),
        P(None, ("seq", "dp"), "tensor"),
        P(None, "tensor"),
        P(None, ("seq", "dp"), "tensor"),
        P(None, ("seq", "dp"), "tensor"),
        P(None, "tensor"),
        P(None, ("seq", "dp"), "tensor"),
        P(),
        P(),
        P(),
        P(None, ("seq", "dp"), "tensor"),
        P(None, "tensor"),
        P(None, ("seq", "dp"), "tensor"),
        P(),
    )
    return jax.shard_map(
        per_device,
        mesh=mesh,
        in_specs=placed,
        out_specs=(
            P("dp", "seq", None),
            P("dp", "seq", None),
            P(),
            P(),
            P(None, ("seq", "dp"), "tensor"),
            P(None, "tensor"),
            P(None, ("seq", "dp"), "tensor"),
            P(None, ("seq", "dp"), "tensor"),
            P(None, "tensor"),
            P(None, ("seq", "dp"), "tensor"),
            P(),
            P(),
            P(),
            P(None, ("seq", "dp"), "tensor"),
            P(None, "tensor"),
            P(None, ("seq", "dp"), "tensor"),
            P(),
        ),
        check_vma=False,
    )
```

```python
import functools
import math

import jax
import jax.numpy as jnp
from jax import lax
from jax.experimental import pallas as pl
from jax.experimental.pallas import tpu as pltpu
from jax.sharding import PartitionSpec as P

HEAD_DIM = 64


EPSILON = 1e-05
INV_ROOT_TWO = 1.0 / math.sqrt(2.0)
INV_ROOT_TWO_PI = 1.0 / math.sqrt(2.0 * math.pi)


def standardize_rows(values):
    center = values - jnp.mean(values, -1, keepdims=True)
    inverse_scale = lax.rsqrt(jnp.mean(center * center, -1, keepdims=True) + EPSILON)
    return (center * inverse_scale, inverse_scale)


def norm_backward_pass(output_gradient, centered_normalized, inverse_scale, norm_gain):
    scaled_values = output_gradient * norm_gain
    return inverse_scale * (
        scaled_values
        - jnp.mean(scaled_values, -1, keepdims=True)
        - centered_normalized * jnp.mean(scaled_values * centered_normalized, -1, keepdims=True)
    )


def times_trans(left, right):
    return lax.dot_general(
        left, right, (((1,), (1,)), ((), ())), preferred_element_type=jnp.float32
    )


def trans_times(left, right):
    return lax.dot_general(
        left, right, (((0,), (0,)), ((), ())), preferred_element_type=jnp.float32
    )


def matmul(left, right):
    return jnp.dot(left, right, preferred_element_type=jnp.float32)


def gelu_slope(pre_act):
    return (
        0.5 * (1.0 + jax.scipy.special.erf(pre_act * INV_ROOT_TWO))
        + pre_act * jnp.exp(-0.5 * pre_act * pre_act) * INV_ROOT_TWO_PI
    )


def attend_forward_kernel(query_ref, pair_ref, out_ref, log_ref):
    cols = query_ref.shape[1]
    scale = HEAD_DIM ** (-0.5)
    query_blk, pair_blk = query_ref[...], pair_ref[...]
    outcomes = []
    for head in range(cols // HEAD_DIM):
        low, high = head * HEAD_DIM, (head + 1) * HEAD_DIM
        scores = times_trans(query_blk[:, low:high], pair_blk[:, low:high]) * scale
        top = jnp.max(scores, -1, keepdims=True)
        expo = jnp.exp(scores - top)
        total = jnp.sum(expo, -1, keepdims=True)
        prob = (expo / total).astype(jnp.bfloat16)
        outcomes.append(matmul(prob, pair_blk[:, cols + low : cols + high]))
        log_ref[head] = top + jnp.log(total)
    out_ref[...] = jnp.concatenate(outcomes, 1).astype(jnp.bfloat16)


def attend_backward_kernel(query_ref, pair_ref, log_ref, grad_ref, grad_query_ref, grad_pair_ref):
    cols = query_ref.shape[1]
    scale = HEAD_DIM ** (-0.5)
    query_blk, pair_blk, grad_blk = query_ref[...], pair_ref[...], grad_ref[...]
    grad_queries, grad_keys, grad_values = [], [], []
    for head in range(cols // HEAD_DIM):
        low, high = head * HEAD_DIM, (head + 1) * HEAD_DIM
        query_head, key_head = query_blk[:, low:high], pair_blk[:, low:high]
        grad_head, value_head = grad_blk[:, low:high], pair_blk[:, cols + low : cols + high]
        scores = times_trans(query_head, key_head) * scale
        prob = jnp.exp(scores - log_ref[head])
        grad_prob = times_trans(grad_head, value_head)
        inner = jnp.sum(prob * grad_prob, -1, keepdims=True)
        grad_scores = (prob * (grad_prob - inner)).astype(jnp.bfloat16)
        grad_queries.append(matmul(grad_scores, key_head) * scale)
        grad_keys.append(trans_times(grad_scores, query_head) * scale)
        grad_values.append(trans_times(prob.astype(jnp.bfloat16), grad_head))
    grad_query_ref[...] = jnp.concatenate(grad_queries, 1).astype(jnp.bfloat16)
    grad_pair_ref[...] = jnp.concatenate(grad_keys + grad_values, 1).astype(jnp.bfloat16)


def attend_forward(query_blk, pair_blk):
    frames, cols = query_blk.shape
    vmem = pl.BlockSpec(memory_space=pltpu.VMEM)
    return pl.pallas_call(
        attend_forward_kernel,
        out_shape=(
            jax.ShapeDtypeStruct((frames, cols), jnp.bfloat16),
            jax.ShapeDtypeStruct((cols // HEAD_DIM, frames, 1), jnp.float32),
        ),
        in_specs=[vmem, vmem],
        out_specs=(vmem, vmem),
        compiler_params=pltpu.CompilerParams(vmem_limit_bytes=32 * 2**20),
        cost_estimate=pl.CostEstimate(
            flops=4 * frames * pair_blk.shape[0] * cols,
            bytes_accessed=15_000_000,
            transcendentals=0,
        ),
        name="attend_forward",
    )(query_blk, pair_blk)


def attend_backward(query_blk, pair_blk, log_total, grad_blk):
    frames, cols = query_blk.shape
    vmem = pl.BlockSpec(memory_space=pltpu.VMEM)
    return pl.pallas_call(
        attend_backward_kernel,
        out_shape=(
            jax.ShapeDtypeStruct((frames, cols), jnp.bfloat16),
            jax.ShapeDtypeStruct(pair_blk.shape, jnp.bfloat16),
        ),
        in_specs=[vmem] * 4,
        out_specs=(vmem, vmem),
        compiler_params=pltpu.CompilerParams(vmem_limit_bytes=32 * 2**20),
        cost_estimate=pl.CostEstimate(
            flops=10 * frames * pair_blk.shape[0] * cols,
            bytes_accessed=20_000_000,
            transcendentals=0,
        ),
        name="attend_backward",
    )(query_blk, pair_blk, log_total, grad_blk)


MESH = pl.DeviceIdType.MESH
PIECES = 4


def tensor_sum_kernel(part_ref, out_ref, got_pair, mid, got_far, tot, got_back, *sems):
    send_a, recv_a, send_b, recv_b, send_c, recv_c = sems
    me = lax.axis_index("tensor")
    core = lax.rem(me, 2)
    pair = me + 1 - 2 * core
    far = lax.rem(me + 2, 4)
    barrier = pltpu.get_barrier_semaphore()
    for other in (pair, far):
        pl.semaphore_signal(barrier, inc=1, device_id={"tensor": other}, device_id_type=MESH)
    pl.semaphore_wait(barrier, 2)
    half = part_ref.shape[0] // 2
    step = half // PIECES
    mine = core * half
    theirs = (1 - core) * half

    def spot(base, piece):
        return pl.ds(pl.multiple_of(base + piece * step, step), step)

    def here(piece):
        return pl.ds(piece * step, step)

    firsts, seconds, thirds = [], [], []
    for piece in range(PIECES):
        copy = pltpu.make_async_remote_copy(
            src_ref=part_ref.at[spot(theirs, piece)],
            dst_ref=got_pair.at[here(piece)],
            send_sem=send_a.at[piece],
            recv_sem=recv_a.at[piece],
            device_id={"tensor": pair},
            device_id_type=MESH,
        )
        copy.start()
        firsts.append(copy)
    for piece in range(PIECES):
        firsts[piece].wait_recv()
        mid[here(piece)] = (
            part_ref[spot(mine, piece)].astype(jnp.float32)
            + got_pair[here(piece)].astype(jnp.float32)
        ).astype(jnp.bfloat16)
        copy = pltpu.make_async_remote_copy(
            src_ref=mid.at[here(piece)],
            dst_ref=got_far.at[here(piece)],
            send_sem=send_b.at[piece],
            recv_sem=recv_b.at[piece],
            device_id={"tensor": far},
            device_id_type=MESH,
        )
        copy.start()
        seconds.append(copy)
    for piece in range(PIECES):
        seconds[piece].wait_recv()
        total = mid[here(piece)].astype(jnp.float32) + got_far[here(piece)].astype(jnp.float32)
        tot[here(piece)] = total
        out_ref[spot(mine, piece)] = total
        copy = pltpu.make_async_remote_copy(
            src_ref=tot.at[here(piece)],
            dst_ref=got_back.at[here(piece)],
            send_sem=send_c.at[piece],
            recv_sem=recv_c.at[piece],
            device_id={"tensor": pair},
            device_id_type=MESH,
        )
        copy.start()
        thirds.append(copy)
    for piece in range(PIECES):
        thirds[piece].wait_recv()
        out_ref[spot(theirs, piece)] = got_back[here(piece)]
    for copy in firsts + seconds + thirds:
        copy.wait_send()


def tensor_sum(partial_value):
    rows, width = partial_value.shape
    half = rows // 2
    return pl.pallas_call(
        tensor_sum_kernel,
        out_shape=jax.ShapeDtypeStruct((rows, width), jnp.float32),
        in_specs=[pl.BlockSpec(memory_space=pltpu.VMEM)],
        out_specs=pl.BlockSpec(memory_space=pltpu.VMEM),
        scratch_shapes=[
            pltpu.VMEM((half, width), jnp.bfloat16),
            pltpu.VMEM((half, width), jnp.bfloat16),
            pltpu.VMEM((half, width), jnp.bfloat16),
            pltpu.VMEM((half, width), jnp.float32),
            pltpu.VMEM((half, width), jnp.float32),
        ]
        + [pltpu.SemaphoreType.DMA((PIECES,))] * 6,
        compiler_params=pltpu.CompilerParams(
            collective_id=0, has_side_effects=True, vmem_limit_bytes=16 * 2**20
        ),
        cost_estimate=pl.CostEstimate(
            flops=rows * width * 4, bytes_accessed=20_000_000, transcendentals=0
        ),
        name="tensor_sum",
    )(partial_value.astype(jnp.bfloat16))


def gather_kernel(seqs, dps, forward, own_ref, out_ref, own_sem, send_z, recv_z, *sems):
    s, d = lax.axis_index("seq"), lax.axis_index("dp")

    def along(k):
        return {"seq": lax.rem(s + k, seqs)}

    def across(j):
        return {"dp": lax.rem(d + j, dps)}

    def slot(k):
        source = lax.rem(s + seqs - k, seqs)
        return source * dps + d if forward else source

    barrier = pltpu.get_barrier_semaphore()
    others = [along(k) for k in range(1, seqs)]
    if forward:
        others += [across(j) for j in range(1, dps)]
    for other in others:
        pl.semaphore_signal(barrier, inc=1, device_id=other, device_id_type=MESH)
    pl.semaphore_wait(barrier, len(others))
    firsts, seconds = [], []
    for k in range(1, seqs):
        copy = pltpu.make_async_remote_copy(
            src_ref=own_ref,
            dst_ref=out_ref.at[slot(0)],
            send_sem=send_z.at[k],
            recv_sem=recv_z.at[k],
            device_id=along(k),
            device_id_type=MESH,
        )
        copy.start()
        firsts.append(copy)
    own = pltpu.make_async_copy(own_ref, out_ref.at[slot(0)], own_sem)
    own.start()
    for k in (0, 1, seqs - 1) + tuple(range(2, seqs - 1)):
        if k:
            firsts[k - 1].wait_recv()
        if forward:
            send_y, recv_y = sems
            for j in range(1, dps):
                copy = pltpu.make_async_remote_copy(
                    src_ref=out_ref.at[slot(k)] if k else own_ref,
                    dst_ref=out_ref.at[slot(k)],
                    send_sem=send_y.at[k * dps + j],
                    recv_sem=recv_y.at[k * dps + j],
                    device_id=across(j),
                    device_id_type=MESH,
                )
                copy.start()
                seconds.append(copy)
    own.wait()
    for copy in firsts:
        copy.wait_send()
    for copy in seconds:
        copy.wait()


def gather_slots(block, forward):
    seqs, dps = lax.axis_size("seq"), lax.axis_size("dp")
    count = seqs * dps if forward else seqs
    sems = [pltpu.SemaphoreType.DMA((seqs,))] * 2
    if forward:
        sems += [pltpu.SemaphoreType.DMA((seqs * dps,))] * 2
    return pl.pallas_call(
        functools.partial(gather_kernel, seqs, dps, forward),
        out_shape=jax.ShapeDtypeStruct((count,) + block.shape, block.dtype),
        in_specs=[pl.BlockSpec(memory_space=pl.ANY)],
        out_specs=pl.BlockSpec(memory_space=pl.ANY),
        scratch_shapes=[pltpu.SemaphoreType.DMA] + sems,
        compiler_params=pltpu.CompilerParams(
            collective_id=2 if forward else 3, has_side_effects=True, vmem_limit_bytes=16 * 2**20
        ),
        cost_estimate=pl.CostEstimate(
            flops=1000, bytes_accessed=100_000_000 if forward else 40_000_000, transcendentals=0
        ),
        name="gather_weights" if forward else "gather_frames",
    )(block)


def frame_sum_kernel(seqs, part_ref, out_ref, got, send_sem, recv_sem):
    s = lax.axis_index("seq")
    barrier = pltpu.get_barrier_semaphore()
    for k in range(1, seqs):
        pl.semaphore_signal(
            barrier, inc=1, device_id={"seq": lax.rem(s + k, seqs)}, device_id_type=MESH
        )
    pl.semaphore_wait(barrier, seqs - 1)
    copies = []
    for k in range(1, seqs):
        other = lax.rem(s + k, seqs)
        copy = pltpu.make_async_remote_copy(
            src_ref=part_ref.at[other],
            dst_ref=got.at[k],
            send_sem=send_sem.at[k],
            recv_sem=recv_sem.at[k],
            device_id={"seq": other},
            device_id_type=MESH,
        )
        copy.start()
        copies.append(copy)
    for copy in copies:
        copy.wait_recv()
    total = part_ref[s].astype(jnp.float32)
    for k in range(1, seqs):
        total = total + got[k].astype(jnp.float32)
    out_ref[...] = total.astype(jnp.bfloat16)
    for copy in copies:
        copy.wait_send()


def frame_sum(parts):
    seqs = lax.axis_size("seq")
    return pl.pallas_call(
        functools.partial(frame_sum_kernel, seqs),
        out_shape=jax.ShapeDtypeStruct(parts.shape[1:], jnp.bfloat16),
        in_specs=[pl.BlockSpec(memory_space=pltpu.VMEM)],
        out_specs=pl.BlockSpec(memory_space=pltpu.VMEM),
        scratch_shapes=[
            pltpu.VMEM(parts.shape, jnp.bfloat16),
            pltpu.SemaphoreType.DMA((seqs,)),
            pltpu.SemaphoreType.DMA((seqs,)),
        ],
        compiler_params=pltpu.CompilerParams(
            collective_id=4, has_side_effects=True, vmem_limit_bytes=16 * 2**20
        ),
        cost_estimate=pl.CostEstimate(flops=1000, bytes_accessed=40_000_000, transcendentals=0),
        name="frame_sum",
    )(parts)


def grad_sum_kernel(
    seqs, dps, part_ref, small_ref, out_ref, small_out, got_y, mid, got_z, slots,
    own_sem, send_s, recv_s, send_y, recv_y, send_z, recv_z,
):
    s, d = lax.axis_index("seq"), lax.axis_index("dp")
    count = seqs * dps
    me = s * dps + d

    def place(shift):
        other = lax.rem(me + shift, count)
        return {"seq": other // dps, "dp": lax.rem(other, dps)}

    barrier = pltpu.get_barrier_semaphore()
    for shift in range(1, count):
        pl.semaphore_signal(barrier, inc=1, device_id=place(shift), device_id_type=MESH)
    pl.semaphore_wait(barrier, count - 1)
    order = tuple(range(1, seqs)) + (0,)
    firsts, seconds, smalls = {}, {}, []
    for k in order:
        for j in range(1, dps):
            to = lax.rem(d + j, dps)
            copy = pltpu.make_async_remote_copy(
                src_ref=part_ref.at[lax.rem(s + k, seqs) * dps + to],
                dst_ref=got_y.at[k * dps + j],
                send_sem=send_y.at[k * dps + j],
                recv_sem=recv_y.at[k * dps + j],
                device_id={"dp": to},
                device_id_type=MESH,
            )
            copy.start()
            firsts[k, j] = copy
    for shift in range(1, count):
        copy = pltpu.make_async_remote_copy(
            src_ref=small_ref,
            dst_ref=slots.at[me],
            send_sem=send_s.at[shift],
            recv_sem=recv_s.at[shift],
            device_id=place(shift),
            device_id_type=MESH,
        )
        copy.start()
        smalls.append(copy)
    own = pltpu.make_async_copy(small_ref, slots.at[me], own_sem)
    own.start()
    for k in order:
        total = part_ref[lax.rem(s + k, seqs) * dps + d].astype(jnp.float32)
        for j in range(1, dps):
            firsts[k, j].wait_recv()
            total = total + got_y[k * dps + j].astype(jnp.float32)
        if k:
            mid[k] = total.astype(jnp.bfloat16)
            copy = pltpu.make_async_remote_copy(
                src_ref=mid.at[k],
                dst_ref=got_z.at[k],
                send_sem=send_z.at[k],
                recv_sem=recv_z.at[k],
                device_id={"seq": lax.rem(s + k, seqs)},
                device_id_type=MESH,
            )
            copy.start()
            seconds[k] = copy
        else:
            out_ref[...] = total
    own.wait()
    for copy in smalls:
        copy.wait()
    total = slots[0]
    for index in range(1, count):
        total = total + slots[index]
    small_out[...] = total
    for k in range(1, seqs):
        seconds[k].wait_recv()
        out_ref[...] = out_ref[...] + got_z[k].astype(jnp.float32)
    for copy in firsts.values():
        copy.wait_send()
    for copy in seconds.values():
        copy.wait_send()


def grad_sum(parts, packed):
    seqs, dps = lax.axis_size("seq"), lax.axis_size("dp")
    count = seqs * dps
    block = parts.shape[1:]
    vmem = pl.BlockSpec(memory_space=pltpu.VMEM)
    return pl.pallas_call(
        functools.partial(grad_sum_kernel, seqs, dps),
        out_shape=(
            jax.ShapeDtypeStruct(block, jnp.float32),
            jax.ShapeDtypeStruct(packed.shape, jnp.float32),
        ),
        in_specs=[vmem, vmem],
        out_specs=(vmem, vmem),
        scratch_shapes=[
            pltpu.VMEM((count,) + block, jnp.bfloat16),
            pltpu.VMEM((seqs,) + block, jnp.bfloat16),
            pltpu.VMEM((seqs,) + block, jnp.bfloat16),
            pltpu.VMEM((count,) + packed.shape, jnp.float32),
            pltpu.SemaphoreType.DMA,
            pltpu.SemaphoreType.DMA((count,)),
            pltpu.SemaphoreType.DMA((count,)),
            pltpu.SemaphoreType.DMA((count,)),
            pltpu.SemaphoreType.DMA((count,)),
            pltpu.SemaphoreType.DMA((seqs,)),
            pltpu.SemaphoreType.DMA((seqs,)),
        ],
        compiler_params=pltpu.CompilerParams(
            collective_id=1, has_side_effects=True, vmem_limit_bytes=32 * 2**20
        ),
        cost_estimate=pl.CostEstimate(flops=1000, bytes_accessed=100_000_000, transcendentals=0),
        name="grad_sum",
    )(parts, packed)


def per_device(
    inputs,
    cotangent,
    attention_norm_gain,
    attention_norm_bias,
    w_query,
    b_query,
    w_key,
    w_value,
    b_value,
    w_out,
    b_out,
    feedforward_norm_gain,
    feedforward_norm_bias,
    w_fc1,
    b_fc1,
    w_fc2,
    b_fc2,
):
    clips, frames_local, width = inputs.shape
    rows = clips * frames_local
    layers = w_query.shape[0]
    cols = w_query.shape[2]
    hidden = w_fc1.shape[2]
    group = ("seq", "dp")
    hidden_state = inputs.astype(jnp.float32).reshape(rows, width)
    full_first, full_rest = [], []
    for layer in range(layers):
        joined = jnp.concatenate(
            [
                w_fc1[layer],
                w_fc2[layer],
                w_query[layer],
                w_key[layer],
                w_value[layer],
                w_out[layer],
            ],
            1,
        )
        if layer == 0:
            whole = gather_slots(joined, True)
            last = whole
            whole = whole.reshape(width, joined.shape[1])
        else:
            joined = joined + last[0, :1, :1] * 0
            whole = lax.all_gather(joined, group, axis=0, tiled=True)
        full_first.append(whole[:, 2 * hidden : 2 * hidden + 3 * cols])
        full_rest.append((whole[:, :hidden], whole[:, hidden : 2 * hidden], whole[:, 2 * hidden + 3 * cols :]))
    saved_all = []
    for layer in range(layers):
        full_qkv = full_first[layer]
        full_up, full_down, full_o = full_rest[layer]
        xhat1, rstd1 = standardize_rows(hidden_state)
        normed1 = (xhat1 * attention_norm_gain[layer] + attention_norm_bias[layer]).astype(
            jnp.bfloat16
        )
        bias = jnp.concatenate([b_query[layer], jnp.zeros_like(b_query[layer]), b_value[layer]])
        qkv = (matmul(normed1, full_qkv) + bias).astype(jnp.bfloat16)
        queries = qkv[:, :cols].reshape(clips, frames_local, cols)
        kv_all = (
            gather_slots(qkv[:, cols:], False)
            .reshape(-1, clips, frames_local, 2 * cols)
            .transpose(1, 0, 2, 3)
            .reshape(clips, -1, 2 * cols)
        )
        outcomes = [
            attend_forward(queries[clip], kv_all[clip])
            for clip in range(clips)
        ]
        log_total = [outcome[1] for outcome in outcomes]
        attended = jnp.concatenate([outcome[0] for outcome in outcomes], 0)
        middle_state = hidden_state + (tensor_sum(times_trans(attended, full_o)) + b_out[layer])
        xhat2, rstd2 = standardize_rows(middle_state)
        normed2 = (xhat2 * feedforward_norm_gain[layer] + feedforward_norm_bias[layer]).astype(
            jnp.bfloat16
        )
        pre_act = matmul(normed2, full_up) + b_fc1[layer]
        activated = jax.nn.gelu(pre_act, approximate=False).astype(jnp.bfloat16)
        hidden_state = middle_state + (
            tensor_sum(times_trans(activated, full_down)) + b_fc2[layer]
        )
        saved_all.append(
            (xhat1, rstd1, normed1, queries, kv_all, log_total, attended, xhat2, rstd2, normed2, pre_act, activated)
        )
    encoded = hidden_state.reshape(clips, frames_local, width)
    state_gradient = cotangent.reshape(rows, width)
    big_grads, smalls = [None] * layers, [None] * layers
    for layer in reversed(range(layers)):
        full_qkv = full_first[layer]
        full_up, full_down, full_o = full_rest[layer]
        (xhat1, rstd1, normed1, queries, kv_all, log_total, attended, xhat2, rstd2, normed2, pre_act, activated) = saved_all[layer]
        grad_mlp = state_gradient.astype(jnp.bfloat16)
        grad_pre = (matmul(grad_mlp, full_down) * gelu_slope(pre_act)).astype(jnp.bfloat16)
        grad_norm2 = tensor_sum(times_trans(grad_pre, full_up))
        middle_gradient = state_gradient + norm_backward_pass(
            grad_norm2, xhat2, rstd2, feedforward_norm_gain[layer]
        )
        grad_attn = middle_gradient.astype(jnp.bfloat16)
        grad_attended = (
            matmul(grad_attn, full_o).astype(jnp.bfloat16).reshape(clips, frames_local, cols)
        )
        outcomes = [
            attend_backward(
                queries[clip],
                kv_all[clip],
                log_total[clip],
                grad_attended[clip],
            )
            for clip in range(clips)
        ]
        kv_terms = jnp.stack([outcome[1] for outcome in outcomes], 0).astype(jnp.bfloat16)
        kv_grads = frame_sum(
            kv_terms.reshape(clips, -1, frames_local, 2 * cols)
            .transpose(1, 0, 2, 3)
            .reshape(-1, rows, 2 * cols)
        )
        grad_query = jnp.concatenate([outcome[0] for outcome in outcomes], 0).astype(jnp.bfloat16)
        grad_qkv = jnp.concatenate([grad_query, kv_grads], 1)
        all_terms = jnp.concatenate(
            [
                trans_times(normed2, grad_pre).astype(jnp.bfloat16),
                trans_times(grad_mlp, activated).astype(jnp.bfloat16),
                trans_times(normed1, grad_qkv).astype(jnp.bfloat16),
                trans_times(grad_attn, attended).astype(jnp.bfloat16),
            ],
            1,
        )
        back_terms = times_trans(grad_qkv, full_qkv).astype(jnp.bfloat16)
        if layer:
            back_terms = back_terms + all_terms[:1, :1] * 0
            big_grads[layer] = lax.psum_scatter(
                all_terms, group, scatter_dimension=0, tiled=True
            ).astype(jnp.float32)
        grad_norm1 = tensor_sum(back_terms)
        state_gradient = middle_gradient + norm_backward_pass(
            grad_norm1, xhat1, rstd1, attention_norm_gain[layer]
        )
        sums_qkv = jnp.sum(grad_qkv, 0, dtype=jnp.float32)
        smalls[layer] = (
            jnp.sum(grad_norm1 * xhat1, 0),
            jnp.sum(grad_norm1, 0),
            sums_qkv[:cols],
            sums_qkv[2 * cols :],
            jnp.sum(grad_attn, 0, dtype=jnp.float32),
            jnp.sum(grad_norm2 * xhat2, 0),
            jnp.sum(grad_norm2, 0),
            jnp.sum(grad_pre, 0, dtype=jnp.float32),
            jnp.sum(grad_mlp, 0, dtype=jnp.float32),
        )
    flat = jnp.concatenate([part for layer in range(layers) for part in smalls[layer]])
    length = flat.shape[0]
    padded = -(-length // 1024) * 1024
    packed = jnp.pad(flat, (0, padded - length)).reshape(padded // 128, 128)
    parts = all_terms.reshape(lax.axis_size(group), -1, all_terms.shape[1])
    big_grads[0], summed = grad_sum(parts, packed)
    summed = summed.reshape(padded)
    small_stack, offset = [[] for _ in range(9)], 0
    for layer in range(layers):
        for member in range(9):
            size = smalls[layer][member].shape[0]
            small_stack[member].append(summed[offset : offset + size])
            offset += size
    small_stack = [jnp.stack(members, 0) for members in small_stack]

    def pick(start, size):
        return jnp.stack([part[:, start : start + size] for part in big_grads], 0)

    grad_inputs = state_gradient.reshape(clips, frames_local, width)
    return (
        encoded,
        grad_inputs,
        small_stack[0],
        small_stack[1],
        pick(2 * hidden, cols),
        small_stack[2],
        pick(2 * hidden + cols, cols),
        pick(2 * hidden + 2 * cols, cols),
        small_stack[3],
        pick(2 * hidden + 3 * cols, cols),
        small_stack[4],
        small_stack[5],
        small_stack[6],
        pick(0, hidden),
        small_stack[7],
        pick(hidden, hidden),
        small_stack[8],
    )


def solution(mesh):
    placed = (
        P("dp", "seq", None),
        P("dp", "seq", None),
        P(),
        P(),
        P(None, ("seq", "dp"), "tensor"),
        P(None, "tensor"),
        P(None, ("seq", "dp"), "tensor"),
        P(None, ("seq", "dp"), "tensor"),
        P(None, "tensor"),
        P(None, ("seq", "dp"), "tensor"),
        P(),
        P(),
        P(),
        P(None, ("seq", "dp"), "tensor"),
        P(None, "tensor"),
        P(None, ("seq", "dp"), "tensor"),
        P(),
    )
    return jax.shard_map(
        per_device,
        mesh=mesh,
        in_specs=placed,
        out_specs=(
            P("dp", "seq", None),
            P("dp", "seq", None),
            P(),
            P(),
            P(None, ("seq", "dp"), "tensor"),
            P(None, "tensor"),
            P(None, ("seq", "dp"), "tensor"),
            P(None, ("seq", "dp"), "tensor"),
            P(None, "tensor"),
            P(None, ("seq", "dp"), "tensor"),
            P(),
            P(),
            P(),
            P(None, ("seq", "dp"), "tensor"),
            P(None, "tensor"),
            P(None, ("seq", "dp"), "tensor"),
            P(),
        ),
        check_vma=False,
    )
```
